32 devices in a mesh: frame: 32 (over z, y, x, core).
Axes of the slice: x: 2, y: 2, z: 4, core: 2. Of those that a mesh axis runs over, the one named last changes fastest.
Arguments:
- diag_even: float32 [64, 256, 256], P('frame'), may hold values from -0.375 to 0.375
- inv_odd: float32 [64, 256, 256], P('frame'), as said below
- coupling: float32 [128, 256, 256], P('frame'), may hold values from -0.375 to 0.375
- arrow_blocks: float32 [128, 512, 256], P('frame'), as said below
- arrow_tip: float32 [512, 512], P('frame'), may hold values from -6 to 6
Outputs:
- diag_new: float32 [64, 256, 256], P('frame')
- couple_new: float32 [64, 256, 256], P('frame')
- arrow_new: float32 [64, 512, 256], P('frame')
- tip_new: float32 [512, 512], P('frame')
The draws below stay inside these ranges and needn't reach their ends.
Inputs may be any that keep to these rules, and one draw needn't show every extreme that they name: `inv_odd`: each block is symmetric, with a diagonal near 1 and small off-diagonal entries. `arrow_blocks`: Real-valued entries of order 256 ** -0.5 or smaller.
All inputs are finite; a program needn't handle non-finite values.
Results may differ from the reference program's by a relative error of at most 0.000076.
Values sent between devices are 32-bit elements; how exact they have to be, the bound alone decides.
A program may use at most 64 MiB of HBM per device.

```python
import jax
import jax.numpy as jnp
from jax import lax

B = 256
A = 512
FR_DEV = 4
FRAMES = 128


def draw_inv_odd(key, part):
    shape = (FRAMES // 2, B, B)
    noise = jax.random.normal(key, shape, jnp.float32)
    sym = 0.5 * (noise + jnp.swapaxes(noise, 1, 2)) / jnp.sqrt(2.0 * B)
    return jnp.eye(B, dtype=jnp.float32)[None] + sym


def draw_arrow_blocks(key, part):
    devices_count = FRAMES // FR_DEV
    key_pattern = jax.random.fold_in(key, 11)
    key_gain = jax.random.fold_in(key, 12)
    key_noise = jax.random.fold_in(key, 13)
    key_pair = jax.random.fold_in(key, 14)
    sigma = 1.0 / jnp.sqrt(jnp.float32(B) * jnp.float32(devices_count))
    pattern = jax.random.truncated_normal(key_pattern, -6.0, 6.0, (A, B), jnp.float32) / jnp.sqrt(jnp.float32(B))
    factor = jnp.exp(jax.random.uniform(key_gain, (FRAMES,), jnp.float32, minval=jnp.log(0.7), maxval=jnp.log(1.4)))
    noise = jax.random.truncated_normal(key_noise, -6.0, 6.0, (FRAMES, A, B), jnp.float32) * sigma
    position = jnp.arange(FRAMES, dtype=jnp.float32)
    rising = jnp.sqrt(1.0 + 2.0 * position / jnp.float32(FRAMES)) * factor
    gains = rising / jnp.sqrt(jnp.float32(FRAMES // 2))
    pairing = jax.random.permutation(key_pair, devices_count).astype(jnp.int32)
    owner = (jnp.arange(FRAMES, dtype=jnp.int32) // FR_DEV).astype(jnp.int32)
    target = pairing[owner]
    row_block = (jnp.arange(A, dtype=jnp.int32) // (A // devices_count)).astype(jnp.int32)
    boost = jnp.where(row_block[None, :] == target[:, None], 3.0, 1.0).astype(jnp.float32)
    blocks = gains[:, None, None] * pattern[None] + noise
    return blocks * boost[:, :, None]


def levels(rng, dims, split, least, high):
    gain, own = 1.0, jax.random.fold_in(rng, 6)
    for axis_at, blocks in split:
        heights = jnp.exp(jax.random.uniform(jax.random.fold_in(own, axis_at), (blocks,), jnp.float32, least / len(split), high / len(split)))
        gain = gain * jnp.repeat(heights, dims[axis_at] // blocks).reshape([-1 if axis == axis_at else 1 for axis in range(len(dims))])
    return gain


def scatter_about(rng, extent, scale, limit, cuts=(), held_as=jnp.bfloat16):
    array = jax.random.normal(rng, extent, jnp.float32) * scale
    if len(cuts) > 0:
        array = levels(rng, extent, cuts, -0.22, 0.18) * array
    return jnp.clip(array, min=-limit, max=limit).astype(held_as)


def setup_inputs(seed: int = 0) -> dict:
    keys = jax.random.split(jax.random.key(seed), 6)
    diag_even = scatter_about(keys[0], (FRAMES // 2, B, B), B ** -0.5, 0.375, ((0, 32),), jnp.float32)
    inv_odd = draw_inv_odd(jax.random.fold_in(keys[5], 71), 0)
    coupling = scatter_about(keys[2], (FRAMES, B, B), B ** -0.5, 0.375, ((0, 32),), jnp.float32)
    arrow_blocks = draw_arrow_blocks(jax.random.fold_in(keys[5], 71), 0)
    arrow_tip = scatter_about(keys[4], (A, A), 0.5, 6.0, ((0, 32),), jnp.float32)
    return {"diag_even": diag_even, "inv_odd": inv_odd, "coupling": coupling, "arrow_blocks": arrow_blocks, "arrow_tip": arrow_tip}


def reference(diag_even, inv_odd, coupling, arrow_blocks, arrow_tip):
    highest = lax.Precision.HIGHEST
    half_count = inv_odd.shape[0]
    order = coupling.shape[1]
    width = arrow_blocks.shape[1]
    linked = coupling.reshape(half_count, 2, order, order)
    link_prev = linked[:, 0]
    link_next = linked[:, 1]
    paired = arrow_blocks.reshape(half_count, 2, width, order)
    arrow_even = paired[:, 0]
    arrow_odd = paired[:, 1]
    left_prod = jnp.matmul(link_prev, inv_odd, precision=highest)
    inv_next = jnp.matmul(inv_odd, link_next, precision=highest)
    arrow_inv = jnp.matmul(arrow_odd, inv_odd, precision=highest)
    diag_left = jnp.matmul(left_prod, jnp.swapaxes(link_prev, 1, 2), precision=highest)
    diag_right = jnp.matmul(jnp.swapaxes(link_next, 1, 2), inv_next, precision=highest)
    couple_new = -jnp.matmul(left_prod, link_next, precision=highest)
    arrow_left = jnp.matmul(arrow_inv, jnp.swapaxes(link_prev, 1, 2), precision=highest)
    arrow_right = jnp.matmul(arrow_odd, inv_next, precision=highest)
    tip_terms = jnp.einsum("hab,hcb->ac", arrow_inv, arrow_odd, precision=highest)
    diag_shift = jnp.concatenate([jnp.zeros((1, order, order), jnp.float32), diag_right[:-1]], axis=0)
    arrow_shift = jnp.concatenate([jnp.zeros((1, width, order), jnp.float32), arrow_right[:-1]], axis=0)
    diag_new = diag_even - diag_left - diag_shift
    arrow_new = arrow_even - arrow_left - arrow_shift
    tip_new = arrow_tip - tip_terms
    return diag_new, couple_new, arrow_new, tip_new
```

```python
import functools
import itertools

import jax
import jax.numpy as jnp
from jax import lax
from jax.experimental import pallas as pl
from jax.experimental.pallas import tpu as pltpu
from jax.sharding import PartitionSpec as P

F32 = jnp.float32
BF16 = jnp.bfloat16
MESH = pl.DeviceIdType.MESH


def shifted(x, axis, by):
    count = lax.axis_size(axis)
    pairs = [(i, i + by) for i in range(count) if 0 <= i + by < count]
    return lax.ppermute(x, axis, pairs)


def product(left, right):
    return jnp.matmul(left, right, precision=lax.Precision.HIGHEST)


def per_device_plain(diag_even, inv_odd, coupling, arrow_blocks, arrow_tip):
    half_count = inv_odd.shape[0]
    order = coupling.shape[1]
    width = arrow_blocks.shape[1]
    linked = coupling.reshape(half_count, 2, order, order)
    link_prev = linked[:, 0]
    link_next = linked[:, 1]
    paired = arrow_blocks.reshape(half_count, 2, width, order)
    arrow_even = paired[:, 0]
    arrow_odd = paired[:, 1]
    left_prod = product(link_prev, inv_odd)
    arrow_inv = product(arrow_odd, inv_odd)
    diag_left = product(left_prod, jnp.swapaxes(link_prev, 1, 2))
    couple_new = -product(left_prod, link_next)
    arrow_left = product(arrow_inv, jnp.swapaxes(link_prev, 1, 2))
    tip_part = jnp.einsum("hab,hcb->ac", arrow_inv, arrow_odd, precision=lax.Precision.HIGHEST)
    inv_next = product(inv_odd, link_next)
    diag_right = product(jnp.swapaxes(link_next, 1, 2), inv_next)
    arrow_right = product(arrow_odd, inv_next)
    recv_diag, recv_arrow = shifted((diag_right[-1], arrow_right[-1]), "frame", 1)
    diag_shift = jnp.concatenate([recv_diag[None], diag_right[:-1]], axis=0)
    arrow_shift = jnp.concatenate([recv_arrow[None], arrow_right[:-1]], axis=0)
    tip_sum = lax.psum_scatter(tip_part, "frame", scatter_dimension=0, tiled=True)
    return (diag_even - diag_left - diag_shift, couple_new, arrow_even - arrow_left - arrow_shift, arrow_tip - tip_sum)


def split(x):
    hi = x.astype(BF16)
    return hi, (x - hi.astype(F32)).astype(BF16)


def stage_plans(bits):
    rest = [(b,) for b in range(1, min(bits, 3))]
    far = [tuple(range(3, bits))] if bits > 3 else []
    first = [(0,)] + rest + far
    second = [(0,)] + rest[1:] + far + rest[:1]
    return [first, second]


def stage_shapes(bits, rows, cols, plan):
    shapes = []
    left = bits
    for group in plan:
        left -= len(group)
        shapes.append((2 ** len(group) - 1,) + (2,) * left + (rows, cols))
    return shapes


def kernel(cfg, diag_ref, inv_ref, coup_ref, arr_ref, tip_ref,
           diag_out, coup_out, arr_out, tip_out,
           diag_v, inv_v, coup_v, arr_v, tip_v,
           m_hi, m_lo, mp_hi, mp_lo, p_hi, p_lo, v_hi, v_lo,
           ar_buf, r_buf, ar_recv, r_recv, ar_mid, r_mid, al_buf, l_buf,
           diag_o, coup_o, arr_o, tip_o, t_buf, *tail):
    n, bits, half, order, width, rows, cols, plans = cfg
    counts = [len(p) for p in plans]
    r_bufs = []
    at = 0
    for c in counts:
        r_bufs.append(tail[at:at + c])
        at += c
    in_sem, out_sem, bs_sem, br_sem, ts_sem, tr_sem = tail[at:]

    me = lax.axis_index("frame")
    bit = [(me // (2 ** b)) % 2 for b in range(bits)]
    nxt = lax.rem(me + 1, n)
    prv = lax.rem(me + n - 1, n)

    def partner(mask):
        other = me
        for b in mask:
            other = other + (1 - 2 * bit[b]) * (2 ** b)
        return other

    def masks(group):
        res = []
        for m in range(1, 2 ** len(group)):
            res.append(tuple(b for i, b in enumerate(group) if (m >> i) & 1))
        return res

    barrier = pltpu.get_barrier_semaphore()
    greet = []
    for group in plans[0]:
        greet += [partner(m) for m in masks(group)]
    greet += [nxt, prv]
    for other in greet:
        pl.semaphore_signal(barrier, inc=1, device_id=(other,), device_id_type=MESH)

    loads = {}
    slot = itertools.count()

    def load(key, src, dst):
        copy = pltpu.make_async_copy(src, dst, in_sem.at[next(slot)])
        copy.start()
        loads[key] = copy

    order_h = list(reversed(range(half)))
    for h in order_h:
        load(("P", h), inv_ref.at[h], inv_v.at[h])
        load(("K", h), arr_ref.at[2 * h + 1], arr_v.at[2 * h + 1])
        if h == half - 1:
            load(("V", h), coup_ref.at[2 * h + 1], coup_v.at[2 * h + 1])
    for h in order_h:
        load(("U", h), coup_ref.at[2 * h], coup_v.at[2 * h])
        if h != half - 1:
            load(("V", h), coup_ref.at[2 * h + 1], coup_v.at[2 * h + 1])
    for h in order_h:
        load(("E", h), arr_ref.at[2 * h], arr_v.at[2 * h])
        load(("D", h), diag_ref.at[h], diag_v.at[h])
    load("tip", tip_ref, tip_v)

    def wait_load(key):
        loads.pop(key).wait()

    K, U, VT = pl.ds(0, width), pl.ds(width, order), pl.ds(width + order, order)

    def put_m(h, rows_at, x):
        m_hi[h, rows_at, :], m_lo[h, rows_at, :] = split(x)

    def cat_l(hi, lo):
        return jnp.concatenate([hi, lo, hi], axis=1)

    def nn(lh, ll, rh, rl):
        return lax.dot_general(cat_l(lh, ll), jnp.concatenate([rh, rh, rl], axis=0),
                               (((1,), (0,)), ((), ())), preferred_element_type=F32)

    def nt(pairs):
        left = jnp.concatenate([cat_l(p[0], p[1]) for p in pairs], axis=1)
        right = jnp.concatenate([jnp.concatenate([p[2], p[2], p[3]], axis=1) for p in pairs], axis=1)
        return lax.dot_general(left, right, (((1,), (1,)), ((), ())), preferred_element_type=F32)

    def get_p(h):
        wait_load(("P", h))
        p_hi[h], p_lo[h] = split(inv_v[h])

    def get_v(h):
        wait_load(("V", h))
        v = coup_v[2 * h + 1]
        v_hi[h], v_lo[h] = split(v)
        put_m(h, VT, v.T)

    def get_k(h):
        wait_load(("K", h))
        put_m(h, K, arr_v[2 * h + 1])

    def get_u(h):
        wait_load(("U", h))
        put_m(h, U, coup_v[2 * h])

    def times_p(h, at):
        mp_hi[h, at, :], mp_lo[h, at, :] = split(nn(m_hi[h, at, :], m_lo[h, at, :], p_hi[h], p_lo[h]))

    def times_v(h, at):
        return nn(mp_hi[h, at, :], mp_lo[h, at, :], v_hi[h], v_lo[h])

    def times_ut(h, at):
        return nt([(mp_hi[h, at, :], mp_lo[h, at, :], m_hi[h, U, :], m_lo[h, U, :])])

    last = half - 1
    get_k(last)
    get_p(last)
    times_p(last, K)
    get_v(last)
    ar_buf[...] = times_v(last, K)
    pl.semaphore_wait(barrier, len(greet))

    def boundary(src, dst, i):
        return pltpu.make_async_remote_copy(src_ref=src, dst_ref=dst, send_sem=bs_sem.at[i], recv_sem=br_sem.at[i],
                                            device_id=(nxt,), device_id_type=MESH)

    send_ar = boundary(ar_buf, ar_recv, 0)
    send_r = boundary(r_buf, r_recv, 1)

    @pl.when(me < n - 1)
    def _():
        send_ar.start()

    times_p(last, VT)
    r_buf[...] = times_v(last, VT)

    @pl.when(me < n - 1)
    def _():
        send_r.start()

    for h in order_h[1:]:
        get_k(h)
        get_p(h)
        times_p(h, K)

    def block_index(done, free, combo):
        idx = [None] * bits
        for b in done:
            idx[b] = bit[b]
        for b, v in zip(free, combo):
            idx[b] = v
        return tuple(reversed(idx))

    sem_at = [0]
    tip_sends = []

    class Chunk:
        def __init__(self, c):
            self.c, self.plan, self.stage, self.done = c, plans[c], 0, []

        def compute(self):
            c = self.c
            at = pl.ds(c * cols, cols)
            part = nt([(mp_hi[h, K, :], mp_lo[h, K, :], m_hi[h, at, :], m_lo[h, at, :]) for h in order_h])
            for d in range(n):
                where = tuple((d >> b) & 1 for b in reversed(range(bits)))
                t_buf[(c,) + where] = part[d * rows:(d + 1) * rows, :]

        def send(self):
            group = self.plan[self.stage]
            self.copies = []
            for i, mask in enumerate(masks(group)):
                idx = [slice(None)] * bits
                for b in self.done:
                    idx[b] = bit[b]
                for b in group:
                    idx[b] = (1 - bit[b]) if b in mask else bit[b]
                copy = pltpu.make_async_remote_copy(
                    src_ref=t_buf.at[(self.c,) + tuple(reversed(idx))],
                    dst_ref=r_bufs[self.c][self.stage].at[i],
                    send_sem=ts_sem.at[sem_at[0]], recv_sem=tr_sem.at[sem_at[0]],
                    device_id=(partner(mask),), device_id_type=MESH)
                sem_at[0] += 1
                copy.start()
                self.copies.append(copy)
                tip_sends.append(copy)

        def receive(self):
            group = self.plan[self.stage]
            self.done = self.done + list(group)
            free = [b for b in range(bits) if b not in self.done]
            for copy in self.copies:
                copy.wait_recv()
            got = r_bufs[self.c][self.stage]
            for combo in itertools.product((0, 1), repeat=len(free)):
                where = (self.c,) + block_index(self.done, free, combo)
                total = t_buf[where]
                for i in range(2 ** len(group) - 1):
                    total = total + got[(i,) + tuple(reversed(combo))]
                t_buf[where] = total
            self.stage += 1
            if self.stage < len(self.plan):
                self.send()

        def finish(self):
            at = pl.ds(self.c * cols, cols)
            tip_o[:, at] = tip_v[:, at] - t_buf[(self.c,) + tuple(reversed(bit))]

    chunks = [Chunk(c) for c in range(len(plans))]
    for chunk in chunks:
        chunk.compute()
        chunk.send()

    stores = []

    def store(src, dst):
        copy = pltpu.make_async_copy(src, dst, out_sem.at[len(stores)])
        copy.start()
        stores.append(copy)

    def couple(h):
        get_u(h)
        times_p(h, U)
        coup_o[h] = -times_v(h, U)
        store(coup_o.at[h], coup_out.at[h])

    def lefts(h):
        al_buf[h] = times_ut(h, K)
        l_buf[h] = times_ut(h, U)

    def rights(h):
        ar_mid[h] = times_v(h, K)
        times_p(h, VT)
        r_mid[h] = times_v(h, VT)

    def combine(h):
        wait_load(("E", h))
        wait_load(("D", h))
        arr_o[h] = arr_v[2 * h] - al_buf[h] - ar_mid[h - 1]
        store(arr_o.at[h], arr_out.at[h])
        diag_o[h] = diag_v[h] - l_buf[h] - r_mid[h - 1]
        store(diag_o.at[h], diag_out.at[h])

    pieces = []
    for h in order_h:
        if h != last:
            pieces.append(functools.partial(get_v, h))
            pieces.append(functools.partial(rights, h))
        pieces.append(functools.partial(couple, h))
        pieces.append(functools.partial(lefts, h))
    for h in order_h[:-1]:
        pieces.append(functools.partial(combine, h))
    steps = [chunk.receive for _ in range(0) for chunk in chunks]
    for s in range(max(counts)):
        steps += [chunk.receive for chunk in chunks if s < len(chunk.plan)]
    while pieces or steps:
        if pieces:
            pieces.pop(0)()
        if steps:
            steps.pop(0)()
    wait_load("tip")
    for chunk in chunks:
        chunk.finish()
    store(tip_o, tip_out)

    wait_load(("E", 0))
    wait_load(("D", 0))
    arr_o[0] = arr_v[0] - al_buf[0]
    diag_o[0] = diag_v[0] - l_buf[0]

    @pl.when(me > 0)
    def _():
        send_ar.wait_recv()
        arr_o[0] = arr_o[0] - ar_recv[...]
        send_r.wait_recv()
        diag_o[0] = diag_o[0] - r_recv[...]

    store(arr_o.at[0], arr_out.at[0])
    store(diag_o.at[0], diag_out.at[0])

    @pl.when(me < n - 1)
    def _():
        send_ar.wait_send()
        send_r.wait_send()

    for copy in tip_sends:
        copy.wait_send()
    for copy in stores:
        copy.wait()


def per_device(n, diag_even, inv_odd, coupling, arrow_blocks, arrow_tip):
    half, order = inv_odd.shape[:2]
    width = arrow_blocks.shape[1]
    rows = arrow_tip.shape[0]
    bits = n.bit_length() - 1
    if 2 ** bits != n or bits < 3 or rows % 8 or width % (2 * 128):
        return per_device_plain(diag_even, inv_odd, coupling, arrow_blocks, arrow_tip)
    plans = stage_plans(bits)
    cols = width // len(plans)
    cfg = (n, bits, half, order, width, rows, cols, plans)
    shapes = [s for plan in plans for s in stage_shapes(bits, rows, cols, plan)]
    copies = sum(2 ** len(g) - 1 for plan in plans for g in plan)
    tall = width + 2 * order
    vmem = pltpu.VMEM
    scratch = [
        vmem(diag_even.shape, F32), vmem(inv_odd.shape, F32), vmem(coupling.shape, F32), vmem(arrow_blocks.shape, F32),
        vmem(arrow_tip.shape, F32),
        vmem((half, tall, order), BF16), vmem((half, tall, order), BF16),
        vmem((half, tall, order), BF16), vmem((half, tall, order), BF16),
        vmem((half, order, order), BF16), vmem((half, order, order), BF16),
        vmem((half, order, order), BF16), vmem((half, order, order), BF16),
        vmem((width, order), F32), vmem((order, order), F32), vmem((width, order), F32), vmem((order, order), F32),
        vmem((half, width, order), F32), vmem((half, order, order), F32),
        vmem((half, width, order), F32), vmem((half, order, order), F32),
        vmem((half, order, order), F32), vmem((half, order, order), F32), vmem((half, width, order), F32),
        vmem(arrow_tip.shape, F32),
        vmem((len(plans),) + (2,) * bits + (rows, cols), F32),
    ]
    scratch += [vmem(s, F32) for s in shapes]
    dma = pltpu.SemaphoreType.DMA
    scratch += [dma((6 * half + 1,)), dma((3 * half + 1,)), dma((2,)), dma((2,)), dma((copies,)), dma((copies,))]
    anywhere = pl.BlockSpec(memory_space=pl.ANY)
    return pl.pallas_call(
        functools.partial(kernel, cfg),
        out_shape=(
            jax.ShapeDtypeStruct((half, order, order), F32),
            jax.ShapeDtypeStruct((half, order, order), F32),
            jax.ShapeDtypeStruct((half, width, order), F32),
            jax.ShapeDtypeStruct(arrow_tip.shape, F32),
        ),
        in_specs=[anywhere] * 5,
        out_specs=(anywhere,) * 4,
        scratch_shapes=scratch,
        compiler_params=pltpu.CompilerParams(collective_id=0, has_side_effects=True, vmem_limit_bytes=48 * 2 ** 20),
        cost_estimate=pl.CostEstimate(flops=90 * 2 * order ** 3, bytes_accessed=6 * 2 ** 20, transcendentals=0),
    )(diag_even, inv_odd, coupling, arrow_blocks, arrow_tip)


def solution(mesh):
    blocks = P("frame", None, None)
    tip = P("frame", None)
    return jax.shard_map(
        functools.partial(per_device, mesh.shape["frame"]),
        mesh=mesh,
        in_specs=(blocks, blocks, blocks, blocks, tip),
        out_specs=(blocks, blocks, blocks, tip),
        check_vma=False,
    )
```

```python
import functools
import itertools

import jax
import jax.numpy as jnp
from jax import lax
from jax.experimental import pallas as pl
from jax.experimental.pallas import tpu as pltpu
from jax.sharding import PartitionSpec as P

F32 = jnp.float32
BF16 = jnp.bfloat16
MESH = pl.DeviceIdType.MESH
AHEAD = 1


def shifted(x, axis, by):
    count = lax.axis_size(axis)
    pairs = [(i, i + by) for i in range(count) if 0 <= i + by < count]
    return lax.ppermute(x, axis, pairs)


def product(left, right):
    return jnp.matmul(left, right, precision=lax.Precision.HIGHEST)


def per_device_plain(diag_even, inv_odd, coupling, arrow_blocks, arrow_tip):
    half_count = inv_odd.shape[0]
    order = coupling.shape[1]
    width = arrow_blocks.shape[1]
    linked = coupling.reshape(half_count, 2, order, order)
    link_prev = linked[:, 0]
    link_next = linked[:, 1]
    paired = arrow_blocks.reshape(half_count, 2, width, order)
    arrow_even = paired[:, 0]
    arrow_odd = paired[:, 1]
    left_prod = product(link_prev, inv_odd)
    arrow_inv = product(arrow_odd, inv_odd)
    diag_left = product(left_prod, jnp.swapaxes(link_prev, 1, 2))
    couple_new = -product(left_prod, link_next)
    arrow_left = product(arrow_inv, jnp.swapaxes(link_prev, 1, 2))
    tip_part = jnp.einsum("hab,hcb->ac", arrow_inv, arrow_odd, precision=lax.Precision.HIGHEST)
    inv_next = product(inv_odd, link_next)
    diag_right = product(jnp.swapaxes(link_next, 1, 2), inv_next)
    arrow_right = product(arrow_odd, inv_next)
    recv_diag, recv_arrow = shifted((diag_right[-1], arrow_right[-1]), "frame", 1)
    diag_shift = jnp.concatenate([recv_diag[None], diag_right[:-1]], axis=0)
    arrow_shift = jnp.concatenate([recv_arrow[None], arrow_right[:-1]], axis=0)
    tip_sum = lax.psum_scatter(tip_part, "frame", scatter_dimension=0, tiled=True)
    return (diag_even - diag_left - diag_shift, couple_new, arrow_even - arrow_left - arrow_shift, arrow_tip - tip_sum)


def split(x):
    hi = x.astype(BF16)
    return hi, (x - hi.astype(F32)).astype(BF16)


def stage_plans(bits):
    core, one, two, far = (0,), (1,), (2,), tuple(range(3, bits))
    return [[core, two, far, one],[core, two, far, one], [core, far, two, one], [core, far, two, one]]


def stage_shapes(bits, rows, cols, plan):
    shapes = []
    left = bits
    for group in plan:
        left -= len(group)
        shapes.append((2 ** len(group) - 1,) + (2,) * left + (rows, cols))
    return shapes


def kernel(cfg, diag_ref, inv_ref, coup_ref, arr_ref, tip_ref,
           diag_o, coup_o, arr_o, tip_o,
           diag_v, inv_v, coup_v, arr_v, tip_v,
           m_hi, m_lo, mp_hi, mp_lo, p_hi, p_lo, v_hi, v_lo,
           ar_buf, r_buf, ar_recv, r_recv, ar_mid, r_mid, al_buf, l_buf,
           t_buf, *tail):
    n, bits, half, order, width, rows, cols, plans = cfg
    counts = [len(p) for p in plans]
    r_bufs = []
    at = 0
    for c in counts:
        r_bufs.append(tail[at:at + c])
        at += c
    in_sem, bs_sem, br_sem, ts_sem, tr_sem = tail[at:]

    me = lax.axis_index("frame")
    bit = [(me // (2 ** b)) % 2 for b in range(bits)]
    nxt = lax.rem(me + 1, n)
    prv = lax.rem(me + n - 1, n)

    def partner(mask):
        other = me
        for b in mask:
            other = other + (1 - 2 * bit[b]) * (2 ** b)
        return other

    def masks(group):
        res = []
        for m in range(1, 2 ** len(group)):
            res.append(tuple(b for i, b in enumerate(group) if (m >> i) & 1))
        return res

    barrier = pltpu.get_barrier_semaphore()
    greet = []
    for mask in sorted({m for plan in plans for group in plan for m in masks(group)}):
        greet.append(partner(mask))
    greet += [nxt, prv]
    for other in greet:
        pl.semaphore_signal(barrier, inc=1, device_id=(other,), device_id_type=MESH)

    loads = {}
    slot = itertools.count()

    def load(key, src, dst):
        copy = pltpu.make_async_copy(src, dst, in_sem.at[next(slot)])
        copy.start()
        loads[key] = copy

    order_h = list(reversed(range(half)))
    for h in order_h:
        load(("P", h), inv_ref.at[h], inv_v.at[h])
        load(("K", h), arr_ref.at[2 * h + 1], arr_v.at[2 * h + 1])
        if h == half - 1:
            load(("V", h), coup_ref.at[2 * h + 1], coup_v.at[2 * h + 1])
    for h in order_h:
        load(("U", h), coup_ref.at[2 * h], coup_v.at[2 * h])
        if h != half - 1:
            load(("V", h), coup_ref.at[2 * h + 1], coup_v.at[2 * h + 1])
    for h in order_h:
        load(("E", h), arr_ref.at[2 * h], arr_v.at[2 * h])
        load(("D", h), diag_ref.at[h], diag_v.at[h])
    load("tip", tip_ref, tip_v)

    def wait_load(key):
        loads.pop(key).wait()

    K, U, VT = pl.ds(0, width), pl.ds(width, order), pl.ds(width + order, order)

    def put_m(h, rows_at, x):
        m_hi[h, rows_at, :], m_lo[h, rows_at, :] = split(x)

    def cat_l(hi, lo):
        return jnp.concatenate([hi, lo, hi], axis=1)

    def nn(lh, ll, rh, rl):
        return lax.dot_general(cat_l(lh, ll), jnp.concatenate([rh, rh, rl], axis=0),
                               (((1,), (0,)), ((), ())), preferred_element_type=F32)

    def nt(pairs):
        left = jnp.concatenate([cat_l(p[0], p[1]) for p in pairs], axis=1)
        right = jnp.concatenate([jnp.concatenate([p[2], p[2], p[3]], axis=1) for p in pairs], axis=1)
        return lax.dot_general(left, right, (((1,), (1,)), ((), ())), preferred_element_type=F32)

    def get_p(h):
        wait_load(("P", h))
        p_hi[h], p_lo[h] = split(inv_v[h])

    def get_v(h):
        wait_load(("V", h))
        v = coup_v[2 * h + 1]
        v_hi[h], v_lo[h] = split(v)
        put_m(h, VT, v.T)

    def get_k(h):
        wait_load(("K", h))
        put_m(h, K, arr_v[2 * h + 1])

    def get_u(h):
        wait_load(("U", h))
        put_m(h, U, coup_v[2 * h])

    def times_p(h, at):
        mp_hi[h, at, :], mp_lo[h, at, :] = split(nn(m_hi[h, at, :], m_lo[h, at, :], p_hi[h], p_lo[h]))

    def times_v(h, at):
        return nn(mp_hi[h, at, :], mp_lo[h, at, :], v_hi[h], v_lo[h])

    def times_ut(h, at):
        return nt([(mp_hi[h, at, :], mp_lo[h, at, :], m_hi[h, U, :], m_lo[h, U, :])])

    last = half - 1
    get_k(last)
    get_p(last)
    times_p(last, K)
    get_v(last)
    ar_buf[...] = times_v(last, K)
    pl.semaphore_wait(barrier, len(greet))

    def boundary(src, dst, i):
        return pltpu.make_async_remote_copy(src_ref=src, dst_ref=dst, send_sem=bs_sem.at[i], recv_sem=br_sem.at[i],
                                            device_id=(nxt,), device_id_type=MESH)

    send_ar = boundary(ar_buf, ar_recv, 0)
    send_r = boundary(r_buf, r_recv, 1)

    @pl.when(me < n - 1)
    def _():
        send_ar.start()

    for h in order_h[1:]:
        get_k(h)
        get_p(h)
        times_p(h, K)

    def block_index(done, free, combo):
        idx = [None] * bits
        for b in done:
            idx[b] = bit[b]
        for b, v in zip(free, combo):
            idx[b] = v
        return tuple(reversed(idx))

    sem_at = [0]
    tip_sends = []

    class Chunk:
        def __init__(self, c):
            self.c, self.plan, self.stage, self.done = c, plans[c], 0, []

        def send(self):
            group = self.plan[self.stage]
            self.copies = []
            for i, mask in enumerate(masks(group)):
                idx = [slice(None)] * bits
                for b in self.done:
                    idx[b] = bit[b]
                for b in group:
                    idx[b] = (1 - bit[b]) if b in mask else bit[b]
                copy = pltpu.make_async_remote_copy(
                    src_ref=t_buf.at[(self.c,) + tuple(reversed(idx))],
                    dst_ref=r_bufs[self.c][self.stage].at[i],
                    send_sem=ts_sem.at[sem_at[0]], recv_sem=tr_sem.at[sem_at[0]],
                    device_id=(partner(mask),), device_id_type=MESH)
                sem_at[0] += 1
                copy.start()
                self.copies.append(copy)
                tip_sends.append(copy)

        def receive(self):
            group = self.plan[self.stage]
            self.done = self.done + list(group)
            free = [b for b in range(bits) if b not in self.done]
            for copy in self.copies:
                copy.wait_recv()
            got = r_bufs[self.c][self.stage]
            for combo in itertools.product((0, 1), repeat=len(free)):
                where = (self.c,) + block_index(self.done, free, combo)
                total = t_buf[where]
                for i in range(2 ** len(group) - 1):
                    total = total + got[(i,) + tuple(reversed(combo))]
                t_buf[where] = total
            self.stage += 1
            if self.stage < len(self.plan):
                self.send()

        def finish(self):
            at = pl.ds(self.c * cols, cols)
            tip_o[:, at] = tip_v[:, at] - t_buf[(self.c,) + tuple(reversed(bit))]

    chunks = [Chunk(c) for c in range(len(plans))]
    wide = max(cols, min(order, width // 2))
    for first in range(0, width, wide):
        at = pl.ds(first, wide)
        part = nt([(mp_hi[h, K, :], mp_lo[h, K, :], m_hi[h, at, :], m_lo[h, at, :]) for h in order_h])
        for c in range(first // cols, (first + wide) // cols):
            here = slice(c * cols - first, (c + 1) * cols - first)
            for d in range(n):
                where = tuple((d >> b) & 1 for b in reversed(range(bits)))
                t_buf[(c,) + where] = part[d * rows:(d + 1) * rows, here]
            chunks[c].send()

    times_p(last, VT)
    r_buf[...] = times_v(last, VT)

    @pl.when(me < n - 1)
    def _():
        send_r.start()

    def couple(h):
        get_u(h)
        times_p(h, U)
        coup_o[h] = -times_v(h, U)

    def lefts(h):
        al_buf[h] = times_ut(h, K)
        l_buf[h] = times_ut(h, U)

    def rights(h):
        ar_mid[h] = times_v(h, K)
        times_p(h, VT)
        r_mid[h] = times_v(h, VT)

    def combine(h):
        wait_load(("E", h))
        wait_load(("D", h))
        arr_o[h] = arr_v[2 * h] - al_buf[h] - ar_mid[h - 1]
        diag_o[h] = diag_v[h] - l_buf[h] - r_mid[h - 1]

    pieces = []
    for h in order_h:
        if h != last:
            pieces.append(functools.partial(get_v, h))
            pieces.append(functools.partial(rights, h))
        pieces.append(functools.partial(couple, h))
        pieces.append(functools.partial(lefts, h))
    for h in order_h[:-1]:
        pieces.append(functools.partial(combine, h))
    steps = []
    for s in range(max(counts)):
        steps += [chunk.receive for chunk in chunks if s < len(chunk.plan)]
    while pieces or steps:
        for _ in range(AHEAD):
            if steps:
                steps.pop(0)()
        if pieces:
            pieces.pop(0)()
    wait_load("tip")
    for chunk in chunks:
        chunk.finish()

    wait_load(("E", 0))
    wait_load(("D", 0))
    arr_o[0] = arr_v[0] - al_buf[0]
    diag_o[0] = diag_v[0] - l_buf[0]

    @pl.when(me > 0)
    def _():
        send_ar.wait_recv()
        arr_o[0] = arr_o[0] - ar_recv[...]
        send_r.wait_recv()
        diag_o[0] = diag_o[0] - r_recv[...]


    @pl.when(me < n - 1)
    def _():
        send_ar.wait_send()
        send_r.wait_send()

    for copy in tip_sends:
        copy.wait_send()


def writer(*refs):
    copies = [pltpu.make_async_copy(refs[i], refs[4 + i], refs[8].at[i]) for i in range(4)]
    for copy in copies:
        copy.start()
    for copy in copies:
        copy.wait()


def per_device(n, diag_even, inv_odd, coupling, arrow_blocks, arrow_tip):
    half, order = inv_odd.shape[:2]
    width = arrow_blocks.shape[1]
    rows = arrow_tip.shape[0]
    bits = n.bit_length() - 1
    if 2 ** bits != n or bits < 4 or rows % 8 or width % (2 * 128):
        return per_device_plain(diag_even, inv_odd, coupling, arrow_blocks, arrow_tip)
    plans = stage_plans(bits)
    cols = width // len(plans)
    cfg = (n, bits, half, order, width, rows, cols, plans)
    shapes = [s for plan in plans for s in stage_shapes(bits, rows, cols, plan)]
    copies = sum(2 ** len(g) - 1 for plan in plans for g in plan)
    tall = width + 2 * order
    vmem = pltpu.VMEM
    scratch = [
        vmem(diag_even.shape, F32), vmem(inv_odd.shape, F32), vmem(coupling.shape, F32), vmem(arrow_blocks.shape, F32),
        vmem(arrow_tip.shape, F32),
        vmem((half, tall, order), BF16), vmem((half, tall, order), BF16),
        vmem((half, tall, order), BF16), vmem((half, tall, order), BF16),
        vmem((half, order, order), BF16), vmem((half, order, order), BF16),
        vmem((half, order, order), BF16), vmem((half, order, order), BF16),
        vmem((width, order), F32), vmem((order, order), F32), vmem((width, order), F32), vmem((order, order), F32),
        vmem((half, width, order), F32), vmem((half, order, order), F32),
        vmem((half, width, order), F32), vmem((half, order, order), F32),
        vmem((len(plans),) + (2,) * bits + (rows, cols), F32),
    ]
    scratch += [vmem(s, F32) for s in shapes]
    dma = pltpu.SemaphoreType.DMA
    scratch += [dma((6 * half + 1,)), dma((2,)), dma((2,)), dma((copies,)), dma((copies,))]
    anywhere = pl.BlockSpec(memory_space=pl.ANY)
    inside = pl.BlockSpec(memory_space=pltpu.VMEM)
    results = pl.pallas_call(
        functools.partial(kernel, cfg),
        out_shape=(
            vmem((half, order, order), F32),
            vmem((half, order, order), F32),
            vmem((half, width, order), F32),
            vmem(arrow_tip.shape, F32),
        ),
        in_specs=[anywhere] * 5,
        out_specs=(inside,) * 4,
        scratch_shapes=scratch,
        compiler_params=pltpu.CompilerParams(collective_id=0, has_side_effects=True, vmem_limit_bytes=48 * 2 ** 20),
        cost_estimate=pl.CostEstimate(flops=90 * 2 * order ** 3, bytes_accessed=6 * 2 ** 20, transcendentals=0),
    )(*[pltpu.with_memory_space_constraint(x, pltpu.HBM)
        for x in (diag_even, inv_odd, coupling, arrow_blocks, arrow_tip)])
    return pl.pallas_call(
        writer,
        out_shape=tuple(pltpu.HBM(r.shape, F32) for r in results),
        in_specs=[inside] * 4,
        out_specs=(anywhere,) * 4,
        scratch_shapes=[dma((4,))],
    )(*[pltpu.with_memory_space_constraint(r, pltpu.VMEM) for r in results])


def solution(mesh):
    blocks = P("frame", None, None)
    tip = P("frame", None)
    return jax.shard_map(
        functools.partial(per_device, mesh.shape["frame"]),
        mesh=mesh,
        in_specs=(blocks, blocks, blocks, blocks, tip),
        out_specs=(blocks, blocks, blocks, tip),
        check_vma=False,
    )
```
